512 devices in a mesh: leaf: 128 (over x, z, core), rank: 4 (over y).
Axes of the slice: x: 4, y: 4, z: 16, core: 2. Of those that a mesh axis runs over, the one named last changes fastest.
Arguments:
- points: float32 [2, 131072], P(None, 'leaf'), may hold values from 0 to 1
- bases: float32 [7, 128, 131072], P(None, 'rank', 'leaf'), may hold values from -1 to 1
- ranks: int32 [7, 128], replicated, may hold values from 64 to 128, as said below
- right_sides: float32 [128, 131072], P('rank', 'leaf'), may hold values from -6 to 6
Outputs:
- solution: float32 [128, 131072], P('rank', 'leaf')
The draws below stay inside these ranges and needn't reach their ends.
Inputs may be any that keep to these rules, and one draw needn't show every extreme that they name: ranks[k, l] is the same for all leaves of one level-k node; in every level one node has rank 128 and another half of 128.
All inputs are finite; a program needn't handle non-finite values.
Results may differ from the reference program's by a relative error of at most 0.00014.
Values sent between devices are 32-bit elements; how exact they have to be, the bound alone decides.
A program may use at most 128 MiB of HBM per device.

```python
import math
import jax
import jax.numpy as jnp
from jax import lax

NL = 1024
R = 128
NB = 128
NLEAF = 128
LEVELS = 7
NPTS = 131072
N_LEAF = 128


def draw_bases(key, part):
    key = jax.random.fold_in(key, 11)
    level = jnp.arange(LEVELS, dtype=jnp.float32)
    spread = (0.75 / jnp.sqrt(NL * jnp.power(2.0, level)))[:, None, None]
    raw = jax.random.truncated_normal(key, -4.0, 4.0, (LEVELS, R, NPTS), jnp.float32)
    return (raw * spread).astype(jnp.float32)


def draw_ranks(key, part):
    key = jax.random.fold_in(key, 23)
    first, second, third = jax.random.split(key, 3)
    leaf = jnp.arange(NLEAF, dtype=jnp.int32)
    level = jnp.arange(LEVELS, dtype=jnp.int32)
    node = jnp.right_shift(leaf[None, :], level[:, None])
    values = jax.random.randint(first, (LEVELS, NLEAF), R // 2, R + 1, dtype=jnp.int32)
    counts = jnp.right_shift(jnp.int32(NLEAF), level)
    highest = jax.random.randint(second, (LEVELS,), 0, NLEAF, dtype=jnp.int32) % counts
    offset = jax.random.randint(third, (LEVELS,), 0, NLEAF, dtype=jnp.int32) % (counts - 1)
    lowest = (highest + 1 + offset) % counts
    table = jnp.take_along_axis(values, node, axis=1)
    table = jnp.where(node == highest[:, None], R, jnp.where(node == lowest[:, None], R // 2, table))
    return table.astype(jnp.int32)


def levels(rng, shape, pieces, smallest, largest):
    loudness, own = 1.0, jax.random.fold_in(rng, 6)
    for position, shards_of in pieces:
        draws = jnp.exp(jax.random.uniform(jax.random.fold_in(own, position), (shards_of,), jnp.float32, smallest / len(pieces), largest / len(pieces)))
        loudness = loudness * jnp.repeat(draws, shape[position] // shards_of).reshape([-1 if axis == position else 1 for axis in range(len(shape))])
    return loudness


def normal_values(stream_key, dims, scale, bound, shards=(), kind=jnp.bfloat16):
    values = jax.random.normal(stream_key, dims, jnp.float32) * scale
    if len(shards) > 0:
        values = levels(stream_key, dims, shards, -0.22, 0.18) * values
    return jnp.clip(values, min=-bound, max=bound).astype(kind)


def setup_inputs(seed: int = 0) -> dict:
    key_list = jax.random.split(jax.random.key(seed), 5)
    return {
        "points": jnp.clip(1.0 * jax.random.uniform(key_list[0], (2, NPTS), jnp.float32) ** levels(key_list[0], (2, NPTS), ((1, 128),), -0.2, 0.2), 0.0, 1.0),
        "bases": draw_bases(jax.random.fold_in(key_list[4], 71), 0),
        "ranks": draw_ranks(jax.random.fold_in(key_list[4], 71), 0),
        "right_sides": normal_values(key_list[3], (NB, NPTS), 1.0, 6.0, ((0, 4), (1, 128)), jnp.float32),
    }


matern_rate = math.sqrt(3.0) / 0.05
nugget = 1.0

def matern_block(coords):
    delta_x = coords[0][:, None] - coords[0][None, :]
    delta_y = coords[1][:, None] - coords[1][None, :]
    distance = jnp.sqrt(delta_x * delta_x + delta_y * delta_y)
    scaled = matern_rate * distance
    return (1.0 + scaled) * jnp.exp(-scaled) + nugget * jnp.eye(coords.shape[1], dtype=jnp.float32)

def couple(gram_own, gram_sib, proj_own, proj_sib, mask_sib):
    exact = lax.Precision.HIGHEST
    system = gram_sib - jnp.matmul(jnp.matmul(gram_sib, gram_own, precision=exact), gram_sib, precision=exact)
    system = system + jnp.diag(1.0 - mask_sib)
    target = jnp.matmul(gram_sib, proj_own - jnp.matmul(gram_own, proj_sib, precision=exact), precision=exact)
    factor = jnp.linalg.cholesky(system)
    remote = jax.scipy.linalg.cho_solve((factor, True), target)
    return proj_sib - jnp.matmul(gram_sib, remote, precision=exact)

def reference(points, bases, ranks, right_sides):
    exact = lax.Precision.HIGHEST
    leaves = N_LEAF
    columns = jnp.arange(R, dtype=jnp.int32)
    mask = (columns[None, None, :] < ranks[:, :, None]).astype(jnp.float32)
    per_leaf = bases.reshape(LEVELS, R, leaves, NL).transpose(2, 0, 1, 3) * mask.transpose(1, 0, 2)[:, :, :, None]
    coords = points.reshape(2, leaves, NL).transpose(1, 0, 2)
    sides = right_sides.reshape(NB, leaves, NL).transpose(1, 0, 2)
    stacked = jnp.concatenate([per_leaf.reshape(leaves, LEVELS * R, NL), sides], axis=1)

    def leaf_solve(pair):
        coord_leaf, rhs_leaf = pair
        factor = jnp.linalg.cholesky(matern_block(coord_leaf))
        return jax.scipy.linalg.cho_solve((factor, True), rhs_leaf.T).T
    solved = lax.map(leaf_solve, (coords, stacked))
    for level_idx in range(LEVELS):
        nodes = leaves >> level_idx
        group = 1 << level_idx
        tilde = solved[:, level_idx * R:(level_idx + 1) * R]
        remaining = solved[:, (level_idx + 1) * R:]
        basis = per_leaf[:, level_idx]
        gram = jnp.einsum('lin,ljn->lij', basis, tilde, precision=exact).reshape(nodes, group, R, R).sum(1)
        proj = jnp.einsum('lin,lcn->lic', basis, remaining, precision=exact)
        proj = proj.reshape((nodes, group) + proj.shape[1:]).sum(1)

        def sibling_of(values):
            return values.reshape((nodes // 2, 2) + values.shape[1:])[:, ::-1].reshape(values.shape)
        node_mask = mask[level_idx].reshape(nodes, group, R)[:, 0]
        weights = jax.vmap(couple)(gram, sibling_of(gram), proj, sibling_of(proj), sibling_of(node_mask))
        weights = jnp.repeat(weights, group, axis=0)
        remaining = remaining - jnp.einsum('lic,lin->lcn', weights, tilde, precision=exact)
        solved = jnp.concatenate([solved[:, :(level_idx + 1) * R], remaining], axis=1)
    result = solved[:, LEVELS * R:]
    return result.transpose(1, 0, 2).reshape(NB, NPTS)
```

```python
import functools
import math

import jax
import jax.numpy as jnp
from jax import lax
from jax.experimental import pallas as pl
from jax.experimental.pallas import tpu as pltpu
from jax.sharding import PartitionSpec as P

matern_rate = math.sqrt(3.0) / 0.05
nugget = 1.0
f32 = jnp.float32
bf16 = jnp.bfloat16
MESH = pl.DeviceIdType.MESH
squarings = (4, 4, 8)


def split(x):
    high = x.astype(bf16)
    return high, (x - high.astype(f32)).astype(bf16)


def dot1(a, b, dims):
    return lax.dot_general(a, b, (dims, ((), ())), preferred_element_type=f32)


def dot3(a, b, dims=((1,), (0,))):
    return dot1(a[0], b[0], dims) + (dot1(a[0], b[1], dims) + dot1(a[1], b[0], dims))


def exact_dot(a, b, dims=((1,), (0,))):
    return lax.dot_general(
        a, b, (dims, ((), ())), precision=lax.Precision.HIGHEST, preferred_element_type=f32
    )


NT = ((1,), (1,))


def identity(n):
    rows = lax.broadcasted_iota(jnp.int32, (n, n), 0)
    return (rows == lax.broadcasted_iota(jnp.int32, (n, n), 1)).astype(f32)


def block_inverse(a, upper, rounds, fixes):
    n = a.shape[0]
    ident = identity(n)
    first = 2.0 / (1.0 + upper)
    width = (upper - 1.0) / (upper + 1.0)
    err = ident - first * a
    x = first * ident
    for _ in range(rounds):
        low = err.astype(bf16)
        both = dot1(jnp.concatenate([x.astype(bf16), low], 0), low, ((1,), (0,)))
        scale = 2.0 / (2.0 - width * width)
        x = scale * (x + both[:n])
        err = scale * both[n:] + (1.0 - scale) * ident
        width = width * width / (2.0 - width * width)
    a_parts = split(a)
    for _ in range(fixes):
        x_parts = split(x)
        residual = ident - dot3(a_parts, x_parts)
        x = x + dot3(x_parts, split(residual))
    return x


def leaf_kernel(block, rows_ref, cols_ref, stacked_ref, matrix_ref, inverse_ref, solved_ref):
    n = matrix_ref.shape[0]
    step = 32

    @pl.loop(0, n // step)
    def _(i):
        start = pl.multiple_of(i * step, step)
        delta_x = cols_ref[pl.ds(start, step), 0:1] - rows_ref[0:1, :]
        delta_y = cols_ref[pl.ds(start, step), 1:2] - rows_ref[1:2, :]
        scaled = matern_rate * jnp.sqrt(delta_x * delta_x + delta_y * delta_y)
        kernel_values = (1.0 + scaled) * jnp.exp(-scaled)
        row_idx = lax.broadcasted_iota(jnp.int32, (step, n), 0) + start
        col_idx = lax.broadcasted_iota(jnp.int32, (step, n), 1)
        values = kernel_values + jnp.where(row_idx == col_idx, nugget, 0.0)
        matrix_ref[pl.ds(start, step), :] = values
        inverse_ref[pl.ds(start, step), :] = values

    count = n // block
    for b in range(count):
        own = slice(b * block, (b + 1) * block)
        pivot = block_inverse(inverse_ref[own, own], 1.0 + block, 6, 2)
        inverse_ref[own, :] = dot3(split(pivot), split(inverse_ref[own, :]))
        inverse_ref[own, own] = pivot
        panel = split(inverse_ref[own, :])
        for i in range(count):
            if i != b:
                other = slice(i * block, (i + 1) * block)
                factor = split(inverse_ref[other, own])
                inverse_ref[other, own] = jnp.zeros((block, block), f32)
                inverse_ref[other, :] = inverse_ref[other, :] - dot3(factor, panel)
    inverse = split(inverse_ref[...])
    first = dot3(split(stacked_ref[...]), inverse)
    residual = stacked_ref[...] - exact_dot(first, matrix_ref[...])
    solved_ref[...] = first + dot3(split(residual), inverse)


def leaf_solve(points, stacked):
    n = points.shape[1]
    return pl.pallas_call(
        functools.partial(leaf_kernel, min(256, n)),
        out_shape=[
            jax.ShapeDtypeStruct((n, n), f32),
            jax.ShapeDtypeStruct((n, n), f32),
            jax.ShapeDtypeStruct(stacked.shape, f32),
        ],
        in_specs=[pl.BlockSpec(memory_space=pltpu.VMEM)] * 3,
        out_specs=[pl.BlockSpec(memory_space=pltpu.VMEM)] * 3,
        compiler_params=pltpu.CompilerParams(vmem_limit_bytes=56 << 20),
        cost_estimate=pl.CostEstimate(flops=10 * n**3, bytes_accessed=16 * n * n, transcendentals=n * n),
    )(points, points.T, stacked)


def gram_kernel(levels, width, solved_ref, basis_ref, out_ref):
    at = 0
    for j in range(levels):
        rows = split(solved_ref[j * width :, :])
        values = dot3(rows, split(basis_ref[j]), NT)
        count = levels + 1 - j
        out_ref[at : at + count] = values.reshape(count, width, values.shape[1])
        at += count


def gram_blocks(solved, basis_full):
    levels, full, n = basis_full.shape
    width = solved.shape[0] // (levels + 1)
    blocks = sum(levels + 1 - j for j in range(levels))
    return pl.pallas_call(
        functools.partial(gram_kernel, levels, width),
        out_shape=jax.ShapeDtypeStruct((blocks, width, full), f32),
        in_specs=[pl.BlockSpec(memory_space=pltpu.VMEM)] * 2,
        out_specs=pl.BlockSpec(memory_space=pltpu.VMEM),
        compiler_params=pltpu.CompilerParams(vmem_limit_bytes=56 << 20),
        cost_estimate=pl.CostEstimate(
            flops=2 * solved.shape[0] * levels * full * n, bytes_accessed=4 * solved.size, transcendentals=0
        ),
    )(solved, basis_full)


def tree_kernel(levels, ranks, width, first_ref, out_ref, *scratch):
    full = ranks * width
    half = width // 2
    starts = [0]
    for j in range(levels):
        starts.append(starts[-1] + levels + 1 - j)
    total = starts[-1]
    current = [first_ref] + list(scratch[: levels - 1])
    arrived = scratch[levels - 1 : 2 * levels - 1]
    own_cols = scratch[2 * levels - 1 : 3 * levels - 1]
    sib_cols = scratch[3 * levels - 1 : 4 * levels - 1]
    weights = scratch[4 * levels - 1 : 5 * levels - 2]
    tail_weights, pair_ref, send_sem, recv_sem = scratch[5 * levels - 2 :]

    leaf = lax.axis_index("leaf")
    rank = lax.axis_index("rank")
    core = leaf % 2
    partners = [leaf + (1 - 2 * ((leaf // (1 << k)) % 2)) * (1 << k) for k in range(levels)]
    peers = [(rank + d) % ranks for d in range(1, ranks)]

    barrier = pltpu.get_barrier_semaphore()
    for p in partners:
        pl.semaphore_signal(barrier, inc=1, device_id={"leaf": p, "rank": rank}, device_id_type=MESH)
    for p in peers:
        pl.semaphore_signal(barrier, inc=1, device_id={"leaf": leaf, "rank": p}, device_id_type=MESH)
    pl.semaphore_wait(barrier, levels + ranks - 1)

    copies = []

    def push(src, dst, to_leaf, to_rank):
        at = len(copies)
        copy = pltpu.make_async_remote_copy(
            src_ref=src,
            dst_ref=dst,
            send_sem=send_sem.at[at],
            recv_sem=recv_sem.at[at],
            device_id={"leaf": to_leaf, "rank": to_rank},
            device_id_type=MESH,
        )
        copy.start()
        copies.append(copy)
        return copy

    def spread(src, dst):
        return [push(src, dst, leaf, p) for p in peers]

    def landed(group):
        for copy in group:
            copy.wait_recv()

    other_core = partners[0]
    mine = pl.ds(core * half, half)
    ident = identity(full)

    for k in range(levels):
        now, sib, own_q, sib_q = current[k], arrived[k], own_cols[k], sib_cols[k]
        base = starts[k]
        inner = levels - k
        blocks = total - base
        after = inner + 1
        after2 = after + (inner if inner > 1 else 0)
        parts = [(0, 1)] + ([(1, inner)] if inner > 1 else [])

        def own_piece(lo, hi):
            if k == 0:
                own_q[lo:hi, pl.ds(rank, 1)] = now[lo:hi][:, None]
            else:
                own_q[lo:hi, pl.ds(rank, 1), mine] = now[lo:hi, mine][:, None]

        if k == 0:
            sent_own = []
            for lo, hi in parts:
                sent_own.append(spread(now.at[lo:hi], own_q.at[lo:hi, rank]))
                own_piece(lo, hi)
            bulk = push(now.at[inner:blocks], sib.at[inner:blocks], partners[0], rank)
            sent_sib = []
            for (lo, hi), group in zip(parts, sent_own):
                landed(group)
                sent_sib.append(push(own_q.at[lo:hi], sib_q.at[lo:hi], partners[0], rank))
            sent_sib[0].wait_recv()
        else:
            sent_far, sent_own = [], []
            for lo, hi in parts:
                sent_far.append(push(now.at[lo:hi, mine], sib.at[lo:hi, mine], partners[k], rank))
                sent_own.append(spread(now.at[lo:hi, mine], own_q.at[lo:hi, rank, mine]))
                own_piece(lo, hi)
            far_next = push(now.at[inner:after2, mine], sib.at[inner:after2, mine], partners[k], rank)
            far_rest = None
            if after2 < blocks:
                far_rest = push(now.at[after2:blocks, mine], sib.at[after2:blocks, mine], partners[k], rank)

            def forward_far(i):
                lo, hi = parts[i]
                sent_far[i].wait_recv()
                group = spread(sib.at[lo:hi, mine], sib_q.at[lo:hi, rank, mine])
                sib_q[lo:hi, pl.ds(rank, 1), mine] = sib[lo:hi, mine][:, None]
                return group

            def share(ref, i):
                lo, hi = parts[i]
                return push(ref.at[lo:hi, :, mine], ref.at[lo:hi, :, mine], other_core, rank)

            groups = [forward_far(0)]
            landed(sent_own[0])
            shared = [share(own_q, 0)]
            landed(groups[0])
            shared.append(share(sib_q, 0))
            landed(shared)

        gram_own = own_q[0].reshape(full, full)
        gram_sib = sib_q[0].reshape(full, full)
        power = exact_dot(gram_sib, gram_own)
        pair_ref[:full] = ident
        pair_ref[full:] = power

        def square(times):
            @pl.loop(0, times)
            def _(_):
                both = exact_dot(pair_ref[...], pair_ref[full:])
                pair_ref[:full] = pair_ref[:full] + both[:full]
                pair_ref[full:] = both[full:]

        square(squarings[0])
        if k == 0:
            square(squarings[1] + squarings[2])
            landed(sent_sib[1:])
            bulk.wait_recv()
        else:
            if inner > 1:
                groups.append(forward_far(1))
                landed(sent_own[1])
                late = [share(own_q, 1)]
            square(squarings[1])
            if inner > 1:
                landed(groups[1])
                late.append(share(sib_q, 1))
            far_next.wait_recv()
            near = [push(sib.at[inner:after2, mine], sib.at[inner:after2, mine], other_core, rank)]
            square(squarings[2])
            if far_rest is not None:
                far_rest.wait_recv()
                near.append(push(sib.at[after2:blocks, mine], sib.at[after2:blocks, mine], other_core, rank))
            if inner > 1:
                landed(late)
            near[0].wait_recv()

        solver = split(pair_ref[:full])
        own_parts, sib_parts = split(gram_own), split(gram_sib)
        proj_own = now[1 : inner + 1].reshape(inner * width, full)
        if inner > 1:
            sib_rows = [sib_q[1:inner, pl.ds(rank, 1)].reshape((inner - 1) * width, full), sib[inner]]
            proj_sib = jnp.concatenate(sib_rows, axis=0)
        else:
            proj_sib = sib[inner]
        target = proj_sib - dot3(split(proj_own), sib_parts)
        z_own = dot3(split(target), solver, NT)
        z_sib = proj_own - dot3(split(z_own), own_parts)
        tail_weights[k] = z_own[(inner - 1) * width :]
        if inner > 1:
            z_both = jnp.concatenate([z_own, z_sib], axis=1)
            after_rows = current[k + 1]
            at = 0
            for j in range(1, inner):
                if j == 2 and k > 0 and far_rest is not None:
                    near[1].wait_recv()
                count = inner + 1 - j
                q_own = own_q[j].reshape(full, full)
                q_sib = sib_q[j].reshape(full, full)
                q_both = jnp.concatenate([q_own, q_sib], axis=1)
                change = dot3(split(z_both[(j - 1) * width :]), split(q_both), NT)
                lo = after + at
                summed = now[lo : lo + count] + sib[lo : lo + count]
                after_rows[at : at + count] = summed - change.reshape(count, width, full)
                at += count
            rows = (inner - 1) * full
            q_own = own_q[1:inner].reshape(rows, full)
            q_sib = sib_q[1:inner].reshape(rows, full)
            wide = q_sib - dot3(split(q_own), sib_parts)
            weights[k][...] = dot3(split(wide), solver, NT)

    for k in reversed(range(levels)):
        value = tail_weights[k]
        for j in range(k + 1, levels):
            block = weights[k][(j - k - 1) * full : (j - k) * full]
            value = value - exact_dot(out_ref[j], block)
        out_ref[k] = value
    for copy in copies:
        copy.wait_send()


def tree_solve(blocks, levels, ranks):
    total, width, full = blocks.shape
    starts = [0]
    for j in range(levels):
        starts.append(starts[-1] + levels + 1 - j)
    scratch = []
    for k in range(1, levels):
        scratch.append(pltpu.VMEM((total - starts[k], width, full), f32))
    for k in range(levels):
        scratch.append(pltpu.VMEM((total - starts[k], width, full), f32))
    for _ in range(2):
        for k in range(levels):
            scratch.append(pltpu.VMEM((levels - k, ranks, width, full), f32))
    for k in range(levels - 1):
        scratch.append(pltpu.VMEM(((levels - k - 1) * full, full), f32))
    scratch.append(pltpu.VMEM((levels, width, full), f32))
    scratch.append(pltpu.VMEM((2 * full, full), f32))
    limit = levels * (4 * (ranks - 1) + 10)
    scratch += [pltpu.SemaphoreType.DMA((limit,)), pltpu.SemaphoreType.DMA((limit,))]
    return pl.pallas_call(
        functools.partial(tree_kernel, levels, ranks, width),
        out_shape=jax.ShapeDtypeStruct((levels, width, full), f32),
        in_specs=[pl.BlockSpec(memory_space=pltpu.VMEM)],
        out_specs=pl.BlockSpec(memory_space=pltpu.VMEM),
        scratch_shapes=scratch,
        compiler_params=pltpu.CompilerParams(
            collective_id=0, has_side_effects=True, vmem_limit_bytes=56 << 20
        ),
    )(blocks)


def local(points, bases, ranks, right_sides):
    high = lax.Precision.HIGH
    levels, width, leaf_pts = bases.shape
    n_ranks = lax.axis_size("rank")
    full = width * n_ranks
    leaf_idx = lax.axis_index("leaf")
    rank_idx = lax.axis_index("rank")
    own_ranks = lax.dynamic_slice_in_dim(ranks, leaf_idx, 1, 1)
    columns = rank_idx * width + jnp.arange(width, dtype=jnp.int32)
    own_mask = (columns[None, :] < own_ranks).astype(f32)
    masked = bases * own_mask[:, :, None]
    basis_full = lax.all_gather(masked, "rank", axis=1, tiled=True)
    stacked = jnp.concatenate([masked.reshape(levels * width, leaf_pts), right_sides], axis=0)
    matrix, inverse, solved = leaf_solve(points, stacked)
    coefs = tree_solve(gram_blocks(solved, basis_full), levels, n_ranks)
    sides = right_sides - jnp.einsum("kci,kin->cn", coefs, basis_full, precision=high)
    first = jnp.matmul(sides, inverse, precision=high)
    residual = sides - jnp.matmul(first, matrix, precision=lax.Precision.HIGHEST)
    return first + jnp.matmul(residual, inverse, precision=high)


def solution(mesh):
    placed = (P(None, "leaf"), P(None, "rank", "leaf"), P(), P("rank", "leaf"))
    return jax.shard_map(
        local, mesh=mesh, in_specs=placed, out_specs=P("rank", "leaf"), check_vma=False
    )
```

```python
import functools
import math

import jax
import jax.numpy as jnp
from jax import lax
from jax.experimental import pallas as pl
from jax.experimental.pallas import tpu as pltpu
from jax.sharding import PartitionSpec as P

matern_rate = math.sqrt(3.0) / 0.05
nugget = 1.0
f32 = jnp.float32
bf16 = jnp.bfloat16
MESH = pl.DeviceIdType.MESH
squarings = (8, 8)
staged = (3, 4)


def split(x):
    high = x.astype(bf16)
    return high, (x - high.astype(f32)).astype(bf16)


def dot1(a, b, dims):
    return lax.dot_general(a, b, (dims, ((), ())), preferred_element_type=f32)


def dot3(a, b, dims=((1,), (0,))):
    return dot1(a[0], b[0], dims) + (dot1(a[0], b[1], dims) + dot1(a[1], b[0], dims))


def exact_dot(a, b, dims=((1,), (0,))):
    return lax.dot_general(
        a, b, (dims, ((), ())), precision=lax.Precision.HIGHEST, preferred_element_type=f32
    )


NT = ((1,), (1,))


def identity(n):
    rows = lax.broadcasted_iota(jnp.int32, (n, n), 0)
    return (rows == lax.broadcasted_iota(jnp.int32, (n, n), 1)).astype(f32)


def block_inverse(a, upper, rounds, fixes):
    n = a.shape[0]
    ident = identity(n)
    first = 2.0 / (1.0 + upper)
    width = (upper - 1.0) / (upper + 1.0)
    err = ident - first * a
    x = first * ident
    for _ in range(rounds):
        low = err.astype(bf16)
        both = dot1(jnp.concatenate([x.astype(bf16), low], 0), low, ((1,), (0,)))
        scale = 2.0 / (2.0 - width * width)
        x = scale * (x + both[:n])
        err = scale * both[n:] + (1.0 - scale) * ident
        width = width * width / (2.0 - width * width)
    a_parts = split(a)
    for _ in range(fixes):
        x_parts = split(x)
        residual = ident - dot3(a_parts, x_parts)
        x = x + dot3(x_parts, split(residual))
    return x


def fill_matrix(points_ref, columns_ref, matrix_ref, inverse_ref):
    n = matrix_ref.shape[0]
    tile = 128
    step = 32
    for axis in range(2):
        for i in range(n // tile):
            row = points_ref[axis : axis + 1, i * tile : (i + 1) * tile]
            columns_ref[axis, i * tile : (i + 1) * tile] = jnp.broadcast_to(row, (tile, tile)).T

    @pl.loop(0, n // step)
    def _(i):
        start = pl.multiple_of(i * step, step)
        own_x = jnp.concatenate([columns_ref[0, pl.ds(start, step)]] * (n // tile), axis=1)
        own_y = jnp.concatenate([columns_ref[1, pl.ds(start, step)]] * (n // tile), axis=1)
        delta_x = own_x - points_ref[0:1, :]
        delta_y = own_y - points_ref[1:2, :]
        scaled = matern_rate * jnp.sqrt(delta_x * delta_x + delta_y * delta_y)
        kernel_values = (1.0 + scaled) * jnp.exp(-scaled)
        row_idx = lax.broadcasted_iota(jnp.int32, (step, n), 0) + start
        col_idx = lax.broadcasted_iota(jnp.int32, (step, n), 1)
        values = kernel_values + jnp.where(row_idx == col_idx, nugget, 0.0)
        matrix_ref[pl.ds(start, step), :] = values
        inverse_ref[pl.ds(start, step), :] = values


def invert(inverse_ref, block):
    count = inverse_ref.shape[0] // block
    for b in range(count):
        own = slice(b * block, (b + 1) * block)
        pivot = block_inverse(inverse_ref[own, own], 1.0 + block, 6, 2)
        inverse_ref[own, :] = dot3(split(pivot), split(inverse_ref[own, :]))
        inverse_ref[own, own] = pivot
        panel = split(inverse_ref[own, :])
        for i in range(count):
            if i != b:
                other = slice(i * block, (i + 1) * block)
                factor = split(inverse_ref[other, own])
                inverse_ref[other, own] = jnp.zeros((block, block), f32)
                inverse_ref[other, :] = inverse_ref[other, :] - dot3(factor, panel)


def refined(sides, inverse, matrix_ref):
    first = dot3(split(sides), inverse)
    residual = sides - exact_dot(first, matrix_ref[...])
    return first + dot3(split(residual), inverse)


def tree_kernel(levels, ranks, width, points_ref, bases_ref, mask_ref, sides_ref, out_ref, *scratch):
    full = ranks * width
    half = width // 2
    starts = [0]
    for j in range(levels):
        starts.append(starts[-1] + levels + 1 - j)
    total = starts[-1]
    current = scratch[:levels]
    arrived = scratch[levels : 2 * levels]
    own_cols = scratch[2 * levels : 3 * levels]
    sib_cols = scratch[3 * levels : 4 * levels]
    weights = scratch[4 * levels : 5 * levels - 1]
    tail_weights, pair_ref, coefs_ref = scratch[5 * levels - 1 : 5 * levels + 2]
    basis_ref, columns_ref, matrix_ref, inverse_ref = scratch[5 * levels + 2 : 5 * levels + 6]
    inverse_high, inverse_low, send_sem, recv_sem = scratch[5 * levels + 6 :]

    leaf = lax.axis_index("leaf")
    rank = lax.axis_index("rank")
    core = leaf % 2
    partners = [leaf + (1 - 2 * ((leaf // (1 << k)) % 2)) * (1 << k) for k in range(levels)]
    peers = [(rank + d) % ranks for d in range(1, ranks)]

    other_core = partners[0]
    known = [(p, rank) for p in partners]
    known += [(leaf, p) for p in peers]
    for k in range(levels):
        if k > 0 and k not in staged:
            known += [(partners[k], p) for p in peers]
    barrier = pltpu.get_barrier_semaphore()
    for to_leaf, to_rank in known:
        pl.semaphore_signal(
            barrier, inc=1, device_id={"leaf": to_leaf, "rank": to_rank}, device_id_type=MESH
        )
    pl.semaphore_wait(barrier, len(known))

    copies = []

    def push(src, dst, to_leaf, to_rank):
        at = len(copies)
        copy = pltpu.make_async_remote_copy(
            src_ref=src,
            dst_ref=dst,
            send_sem=send_sem.at[at],
            recv_sem=recv_sem.at[at],
            device_id={"leaf": to_leaf, "rank": to_rank},
            device_id_type=MESH,
        )
        copy.start()
        copies.append(copy)
        return copy

    def spread(src, dst):
        return [push(src, dst, leaf, p) for p in peers]

    def spread_chip(src, dst):
        group = [push(src, dst, other_core, rank)]
        for p in peers:
            group += [push(src, dst, leaf, p), push(src, dst, other_core, p)]
        return group

    def landed(group):
        for copy in group:
            copy.wait_recv()

    mine = pl.ds(core * half, half)
    ident = identity(full)
    moves = [dict() for _ in range(levels)]

    def shape_of(k):
        inner = levels - k
        after = inner + 1
        return inner, after, after + (inner if inner > 1 else 0), total - starts[k]

    def begin_column(k):
        now, sib, own_q, sib_q, move = current[k], arrived[k], own_cols[k], sib_cols[k], moves[k]
        inner = levels - k
        move["own"] = spread(now.at[0:1], own_q.at[0:1, rank])
        if k in staged:
            move["far_gram"] = push(now.at[0:1, mine], sib_q.at[0:1, rank, mine], partners[k], rank)
        else:
            move["gram"] = [push(now.at[0:1], sib_q.at[0:1, rank], partners[k], rank)]
            move["gram"] += [push(now.at[0:1], sib_q.at[0:1, rank], partners[k], p) for p in peers]
        own_q[0:inner, pl.ds(rank, 1)] = now[0:inner][:, None]
        move["own_rest"] = []
        if inner > 1:
            if k > 0:
                move["far_rest"] = push(
                    now.at[1:inner, mine], sib_q.at[1:inner, rank, mine], partners[k], rank
                )
            move["own_rest"] = spread(now.at[1:inner], own_q.at[1:inner, rank])

    def begin_rest(k):
        now, sib, move = current[k], arrived[k], moves[k]
        inner, after, after2, blocks = shape_of(k)
        if k == 0:
            move["bulk"] = push(now.at[inner:blocks], sib.at[inner:blocks], partners[0], rank)
            return
        move["far"] = []
        for lo, hi in ((inner, after2), (after2, blocks)):
            if lo < hi:
                move["far"].append(push(now.at[lo:hi, mine], sib.at[lo:hi, mine], partners[k], rank))

    def share_far(k, i):
        sib, move = arrived[k], moves[k]
        inner, after, after2, blocks = shape_of(k)
        lo, hi = ((inner, after2), (after2, blocks))[i]
        move["far"][i].wait_recv()
        return push(sib.at[lo:hi, mine], sib.at[lo:hi, mine], other_core, rank)

    basis_ref[:, pl.ds(rank, 1)] = (bases_ref[...] * mask_ref[...])[:, None]
    gathered = spread(basis_ref.at[:, rank], basis_ref.at[:, rank])
    n = matrix_ref.shape[0]
    fill_matrix(points_ref, columns_ref, matrix_ref, inverse_ref)
    invert(inverse_ref, min(256, n))
    inverse_high[...], inverse_low[...] = split(inverse_ref[...])
    inverse = (inverse_high[...], inverse_low[...])
    landed(gathered)
    later = basis_ref[1:, pl.ds(rank, 1)].reshape((levels - 1) * width, n)
    stacked = jnp.concatenate([basis_ref[0].reshape(full, n), later, sides_ref[...]], axis=0)
    solved = refined(stacked, inverse, matrix_ref)
    basis_parts = split(basis_ref[...].reshape(levels * full, n))
    column = dot3(basis_parts, split(solved[:full]), NT)
    own_cols[0][...] = column.reshape(levels, ranks, width, full)
    moves[0]["gram"] = [push(own_cols[0].at[0:1], sib_cols[0].at[0:1], other_core, rank)]
    moves[0]["rest"] = []
    if levels > 1:
        moves[0]["rest"] = [push(own_cols[0].at[1:levels], sib_cols[0].at[1:levels], other_core, rank)]
    current[0][0:levels] = own_cols[0][:, pl.ds(rank, 1)].reshape(levels, width, full)
    solved_parts = split(solved[full:])
    at = levels
    for j in range(levels):
        count = levels + 1 - j if j else 1
        rows = levels * width - count * width
        left = (solved_parts[0][rows:], solved_parts[1][rows:])
        right = (basis_parts[0][j * full : (j + 1) * full], basis_parts[1][j * full : (j + 1) * full])
        current[0][at : at + count] = dot3(left, right, NT).reshape(count, width, full)
        at += count
    begin_rest(0)
    for k in range(levels):
        now, sib, own_q, sib_q, move = current[k], arrived[k], own_cols[k], sib_cols[k], moves[k]
        inner, after, after2, blocks = shape_of(k)
        rest = []
        if k in staged:
            move["far_gram"].wait_recv()
            move["gram"] = spread_chip(sib_q.at[0:1, rank, mine], sib_q.at[0:1, rank, mine])
        if k > 0 and inner > 1:
            move["far_rest"].wait_recv()
            rest = spread_chip(sib_q.at[1:inner, rank, mine], sib_q.at[1:inner, rank, mine])
        landed(move.get("own", []))
        landed(move["gram"])

        gram_own = own_q[0].reshape(full, full)
        gram_sib = sib_q[0].reshape(full, full)
        pair_ref[:full] = ident
        pair_ref[full:] = exact_dot(gram_sib, gram_own)

        def square(times):
            @pl.loop(0, times)
            def _(_):
                both = exact_dot(pair_ref[...], pair_ref[full:])
                pair_ref[:full] = pair_ref[:full] + both[:full]
                pair_ref[full:] = both[full:]

        square(squarings[0])
        landed(move.get("own_rest", []))
        near = []
        if k == 0:
            rest = move["rest"]
        else:
            near.append(share_far(k, 0))
        square(squarings[1])
        if k > 0 and after2 < blocks:
            near.append(share_far(k, 1))
        landed(rest)
        if k == 0:
            move["bulk"].wait_recv()
        else:
            near[0].wait_recv()

        solver = split(pair_ref[:full])
        own_parts, sib_parts = split(gram_own), split(gram_sib)
        proj_own = now[1 : inner + 1].reshape(inner * width, full)
        if inner > 1:
            sib_rows = [sib_q[1:inner, pl.ds(rank, 1)].reshape((inner - 1) * width, full), sib[inner]]
            proj_sib = jnp.concatenate(sib_rows, axis=0)
        else:
            proj_sib = sib[inner]
        target = proj_sib - dot3(split(proj_own), sib_parts)
        z_own = dot3(split(target), solver, NT)
        tail_weights[k] = z_own[(inner - 1) * width :]
        if inner > 1:
            z_sib = proj_own - dot3(split(z_own), own_parts)
            z_both = jnp.concatenate([z_own, z_sib], axis=1)
            after_rows = current[k + 1]
            at = 0
            for j in range(1, inner):
                if j == 2 and k > 0 and after2 < blocks:
                    near[1].wait_recv()
                count = inner + 1 - j
                q_own = own_q[j].reshape(full, full)
                q_sib = sib_q[j].reshape(full, full)
                q_both = jnp.concatenate([q_own, q_sib], axis=1)
                change = dot3(split(z_both[(j - 1) * width :]), split(q_both), NT)
                lo = after + at
                summed = now[lo : lo + count] + sib[lo : lo + count]
                after_rows[at : at + count] = summed - change.reshape(count, width, full)
                at += count
                if j == 1:
                    begin_column(k + 1)
            begin_rest(k + 1)
            rows = (inner - 1) * full
            q_own = own_q[1:inner].reshape(rows, full)
            q_sib = sib_q[1:inner].reshape(rows, full)
            wide = q_sib - dot3(split(q_own), sib_parts)
            weights[k][...] = dot3(split(wide), solver, NT)

    for k in reversed(range(levels)):
        value = tail_weights[k]
        for j in range(k + 1, levels):
            block = weights[k][(j - k - 1) * full : (j - k) * full]
            value = value - exact_dot(coefs_ref[j], block)
        coefs_ref[k] = value
    coefs = jnp.concatenate([coefs_ref[k] for k in range(levels)], axis=1)
    basis_parts = split(basis_ref[...].reshape(levels * full, n))
    sides = sides_ref[...] - dot3(split(coefs), basis_parts)
    out_ref[...] = refined(sides, (inverse_high[...], inverse_low[...]), matrix_ref)
    for copy in copies:
        copy.wait_send()


def tree_solve(points, bases, mask, right_sides, ranks):
    levels, width, n = bases.shape
    full = width * ranks
    starts = [0]
    for j in range(levels):
        starts.append(starts[-1] + levels + 1 - j)
    total = starts[-1]
    scratch = []
    for _ in range(2):
        for k in range(levels):
            scratch.append(pltpu.VMEM((total - starts[k], width, full), f32))
    for _ in range(2):
        for k in range(levels):
            scratch.append(pltpu.VMEM((levels - k, ranks, width, full), f32))
    for k in range(levels - 1):
        scratch.append(pltpu.VMEM(((levels - k - 1) * full, full), f32))
    scratch += [
        pltpu.VMEM((levels, width, full), f32),
        pltpu.VMEM((2 * full, full), f32),
        pltpu.VMEM((levels, width, full), f32),
        pltpu.VMEM((levels, ranks, width, n), f32),
        pltpu.VMEM((2, n, 128), f32),
        pltpu.VMEM((n, n), f32),
        pltpu.VMEM((n, n), f32),
        pltpu.VMEM((n, n), bf16),
        pltpu.VMEM((n, n), bf16),
    ]
    limit = levels * 7 * ranks
    scratch += [pltpu.SemaphoreType.DMA((limit,)), pltpu.SemaphoreType.DMA((limit,))]
    return pl.pallas_call(
        functools.partial(tree_kernel, levels, ranks, width),
        out_shape=jax.ShapeDtypeStruct(right_sides.shape, f32),
        in_specs=[pl.BlockSpec(memory_space=pltpu.VMEM)] * 4,
        out_specs=pl.BlockSpec(memory_space=pltpu.VMEM),
        scratch_shapes=scratch,
        compiler_params=pltpu.CompilerParams(
            collective_id=0, has_side_effects=True, vmem_limit_bytes=60 << 20
        ),
    )(points, bases, mask, right_sides)


def local(points, bases, ranks, right_sides):
    width = bases.shape[1]
    n_ranks = lax.axis_size("rank")
    leaf_idx = lax.axis_index("leaf")
    rank_idx = lax.axis_index("rank")
    own_ranks = lax.dynamic_slice_in_dim(ranks, leaf_idx, 1, 1)
    columns = rank_idx * width + jnp.arange(width, dtype=jnp.int32)
    own_mask = (columns[None, :] < own_ranks).astype(f32)
    return tree_solve(points, bases, own_mask[:, :, None], right_sides, n_ranks)


def solution(mesh):
    placed = (P(None, "leaf"), P(None, "rank", "leaf"), P(), P("rank", "leaf"))
    return jax.shard_map(
        local, mesh=mesh, in_specs=placed, out_specs=P("rank", "leaf"), check_vma=False
    )
```

```python
import functools
import math

import jax
import jax.numpy as jnp
from jax import lax
from jax.experimental import pallas as pl
from jax.experimental.pallas import tpu as pltpu
from jax.sharding import PartitionSpec as P

matern_rate = math.sqrt(3.0) / 0.05
nugget = 1.0
f32 = jnp.float32
bf16 = jnp.bfloat16
MESH = pl.DeviceIdType.MESH
squarings = (8, 8)
staged = (3, 4)


def split(x):
    high = x.astype(bf16)
    return high, (x - high.astype(f32)).astype(bf16)


def dot1(a, b, dims):
    return lax.dot_general(a, b, (dims, ((), ())), preferred_element_type=f32)


def dot3(a, b, dims=((1,), (0,))):
    return dot1(a[0], b[0], dims) + (dot1(a[0], b[1], dims) + dot1(a[1], b[0], dims))


def exact_dot(a, b, dims=((1,), (0,))):
    return lax.dot_general(
        a, b, (dims, ((), ())), precision=lax.Precision.HIGHEST, preferred_element_type=f32
    )


NT = ((1,), (1,))


def identity(n):
    rows = lax.broadcasted_iota(jnp.int32, (n, n), 0)
    return (rows == lax.broadcasted_iota(jnp.int32, (n, n), 1)).astype(f32)


def block_inverse(a, upper, rounds, fixes):
    n = a.shape[0]
    ident = identity(n)
    first = 2.0 / (1.0 + upper)
    width = (upper - 1.0) / (upper + 1.0)
    err = ident - first * a
    x = first * ident
    for _ in range(rounds):
        low = err.astype(bf16)
        both = dot1(jnp.concatenate([x.astype(bf16), low], 0), low, ((1,), (0,)))
        scale = 2.0 / (2.0 - width * width)
        x = scale * (x + both[:n])
        err = scale * both[n:] + (1.0 - scale) * ident
        width = width * width / (2.0 - width * width)
    a_parts = split(a)
    for _ in range(fixes):
        x_parts = split(x)
        residual = ident - dot3(a_parts, x_parts)
        x = x + dot3(x_parts, split(residual))
    return x


def fill_matrix(points_ref, columns_ref, matrix_ref, inverse_ref):
    n = matrix_ref.shape[0]
    tile = 128
    step = 32
    for axis in range(2):
        for i in range(n // tile):
            row = points_ref[axis : axis + 1, i * tile : (i + 1) * tile]
            columns_ref[axis, i * tile : (i + 1) * tile] = jnp.broadcast_to(row, (tile, tile)).T

    @pl.loop(0, n // step)
    def _(i):
        start = pl.multiple_of(i * step, step)
        own_x = jnp.concatenate([columns_ref[0, pl.ds(start, step)]] * (n // tile), axis=1)
        own_y = jnp.concatenate([columns_ref[1, pl.ds(start, step)]] * (n // tile), axis=1)
        delta_x = own_x - points_ref[0:1, :]
        delta_y = own_y - points_ref[1:2, :]
        scaled = matern_rate * jnp.sqrt(delta_x * delta_x + delta_y * delta_y)
        kernel_values = (1.0 + scaled) * jnp.exp(-scaled)
        row_idx = lax.broadcasted_iota(jnp.int32, (step, n), 0) + start
        col_idx = lax.broadcasted_iota(jnp.int32, (step, n), 1)
        values = kernel_values + jnp.where(row_idx == col_idx, nugget, 0.0)
        matrix_ref[pl.ds(start, step), :] = values
        inverse_ref[pl.ds(start, step), :] = values


def invert(inverse_ref, block, last_step):
    count = inverse_ref.shape[0] // block
    for b in range(count):
        if b == count - 1:
            last_step()
        own = slice(b * block, (b + 1) * block)
        pivot = block_inverse(inverse_ref[own, own], 1.0 + block, 6, 2)
        inverse_ref[own, :] = dot3(split(pivot), split(inverse_ref[own, :]))
        inverse_ref[own, own] = pivot
        panel = split(inverse_ref[own, :])
        for i in range(count):
            if i != b:
                other = slice(i * block, (i + 1) * block)
                factor = split(inverse_ref[other, own])
                inverse_ref[other, own] = jnp.zeros((block, block), f32)
                inverse_ref[other, :] = inverse_ref[other, :] - dot3(factor, panel)


def refined(sides, inverse, matrix_ref):
    first = dot3(split(sides), inverse)
    residual = sides - exact_dot(first, matrix_ref[...])
    return first + dot1(residual.astype(bf16), inverse[0], ((1,), (0,)))


def tree_kernel(levels, ranks, width, points_ref, bases_ref, mask_ref, sides_ref, out_ref, *scratch):
    full = ranks * width
    half = width // 2
    starts = [0]
    for j in range(levels):
        starts.append(starts[-1] + levels + 1 - j)
    total = starts[-1]
    current = scratch[:levels]
    arrived = scratch[levels : 2 * levels]
    own_cols = scratch[2 * levels : 3 * levels]
    sib_cols = scratch[3 * levels : 4 * levels]
    weights = scratch[4 * levels : 5 * levels - 1]
    tail_weights, pair_ref, coefs_ref = scratch[5 * levels - 1 : 5 * levels + 2]
    basis_ref, columns_ref, matrix_ref, inverse_ref = scratch[5 * levels + 2 : 5 * levels + 6]
    inverse_high, inverse_low, solved_ref, solved_sides, send_sem, recv_sem = scratch[5 * levels + 6 :]

    leaf = lax.axis_index("leaf")
    rank = lax.axis_index("rank")
    core = leaf % 2
    partners = [leaf + (1 - 2 * ((leaf // (1 << k)) % 2)) * (1 << k) for k in range(levels)]
    peers = [(rank + d) % ranks for d in range(1, ranks)]

    other_core = partners[0]
    known = [(p, rank) for p in partners]
    known += [(leaf, p) for p in peers]
    for k in range(levels):
        if k == 0 or k not in staged:
            known += [(partners[k], p) for p in peers]
    barrier = pltpu.get_barrier_semaphore()
    for to_leaf, to_rank in known:
        pl.semaphore_signal(
            barrier, inc=1, device_id={"leaf": to_leaf, "rank": to_rank}, device_id_type=MESH
        )
    pl.semaphore_wait(barrier, len(known))

    copies = []

    def push(src, dst, to_leaf, to_rank):
        at = len(copies)
        copy = pltpu.make_async_remote_copy(
            src_ref=src,
            dst_ref=dst,
            send_sem=send_sem.at[at],
            recv_sem=recv_sem.at[at],
            device_id={"leaf": to_leaf, "rank": to_rank},
            device_id_type=MESH,
        )
        copy.start()
        copies.append(copy)
        return copy

    def spread(src, dst):
        return [push(src, dst, leaf, p) for p in peers]

    def spread_chip(src, dst):
        group = [push(src, dst, other_core, rank)]
        for p in peers:
            group += [push(src, dst, leaf, p), push(src, dst, other_core, p)]
        return group

    def landed(group):
        for copy in group:
            copy.wait_recv()

    mine = pl.ds(core * half, half)
    ident = identity(full)
    moves = [dict() for _ in range(levels)]

    def shape_of(k):
        inner = levels - k
        after = inner + 1
        return inner, after, after + (inner if inner > 1 else 0), total - starts[k]

    def begin_column(k):
        now, sib, own_q, sib_q, move = current[k], arrived[k], own_cols[k], sib_cols[k], moves[k]
        inner = levels - k
        move["own"] = spread(now.at[0:1], own_q.at[0:1, rank])
        if k in staged:
            move["far_gram"] = push(now.at[0:1, mine], sib_q.at[0:1, rank, mine], partners[k], rank)
        else:
            move["gram"] = [push(now.at[0:1], sib_q.at[0:1, rank], partners[k], rank)]
            move["gram"] += [push(now.at[0:1], sib_q.at[0:1, rank], partners[k], p) for p in peers]
        own_q[0:1, pl.ds(rank, 1)] = now[0:1][:, None]
        move["own_rest"] = []
        if inner > 1:
            own_q[1:inner, pl.ds(rank, 1), mine] = now[1:inner, mine][:, None]
            if k > 0:
                move["far_rest"] = push(
                    now.at[1:inner, mine], sib_q.at[1:inner, rank, mine], partners[k], rank
                )
            move["own_rest"] = spread(now.at[1:inner, mine], own_q.at[1:inner, rank, mine])

    def begin_rest(k):
        now, sib, move = current[k], arrived[k], moves[k]
        inner, after, after2, blocks = shape_of(k)
        if k == 0:
            move["bulk"] = push(now.at[inner:blocks], sib.at[inner:blocks], partners[0], rank)
            return
        move["far"] = []
        for lo, hi in ((inner, after2), (after2, blocks)):
            if lo < hi:
                move["far"].append(push(now.at[lo:hi, mine], sib.at[lo:hi, mine], partners[k], rank))

    def share_far(k, i):
        sib, move = arrived[k], moves[k]
        inner, after, after2, blocks = shape_of(k)
        lo, hi = ((inner, after2), (after2, blocks))[i]
        move["far"][i].wait_recv()
        return push(sib.at[lo:hi, mine], sib.at[lo:hi, mine], other_core, rank)

    basis_ref[:, pl.ds(rank, 1)] = (bases_ref[...] * mask_ref[...])[:, None]
    right, left = peers[0], peers[-1]
    middle = 1 + levels // 2
    lead, early, late = slice(0, 1), slice(1, middle), slice(middle, levels)

    def pass_on(part, source, to):
        return [push(basis_ref.at[part, source], basis_ref.at[part, source], leaf, to)]

    lead_right, lead_left = pass_on(lead, rank, right), pass_on(lead, rank, left)
    early_right, late_left = pass_on(early, rank, right), pass_on(late, rank, left)
    late_right, early_left = pass_on(late, rank, right), pass_on(early, rank, left)
    lead_group, rest_group = [], []

    def relay():
        landed(lead_right)
        lead_group.extend(lead_left + pass_on(lead, left, right))
        landed(early_right)
        rest_group.extend(late_right + pass_on(early, left, right))
        landed(late_left)
        rest_group.extend(early_left + pass_on(late, right, left))

    n = matrix_ref.shape[0]
    fill_matrix(points_ref, columns_ref, matrix_ref, inverse_ref)
    invert(inverse_ref, min(256, n), relay)
    inverse_high[...], inverse_low[...] = split(inverse_ref[...])
    inverse = (inverse_high[...], inverse_low[...])
    later = basis_ref[1:, pl.ds(rank, 1)].reshape((levels - 1) * width, n)
    solved_later = refined(jnp.concatenate([later, sides_ref[...]], axis=0), inverse, matrix_ref)
    solved_sides[...] = solved_later[(levels - 1) * width :]
    landed(lead_group)
    solved_ref[0] = refined(basis_ref[0].reshape(full, n), inverse, matrix_ref)
    landed(rest_group)
    basis_parts = split(basis_ref[...].reshape(levels * full, n))
    column = dot3(basis_parts, split(solved_ref[0]), NT)
    own_cols[0][...] = column.reshape(levels, ranks, width, full)
    moves[0]["gram"] = [push(own_cols[0].at[0:1], sib_cols[0].at[0:1], other_core, rank)]
    moves[0]["rest"] = []
    if levels > 1:
        moves[0]["rest"] = [push(own_cols[0].at[1:levels], sib_cols[0].at[1:levels], other_core, rank)]
    current[0][0:levels] = own_cols[0][:, pl.ds(rank, 1)].reshape(levels, width, full)
    solved_parts = split(solved_later)
    at = levels
    for j in range(levels):
        count = levels + 1 - j if j else 1
        rows = levels * width - count * width
        left = (solved_parts[0][rows:], solved_parts[1][rows:])
        right = (basis_parts[0][j * full : (j + 1) * full], basis_parts[1][j * full : (j + 1) * full])
        current[0][at : at + count] = dot3(left, right, NT).reshape(count, width, full)
        at += count
    begin_rest(0)
    for k in range(levels):
        now, sib, own_q, sib_q, move = current[k], arrived[k], own_cols[k], sib_cols[k], moves[k]
        inner, after, after2, blocks = shape_of(k)
        rest = []
        if k > 0:
            inverse = (inverse_high[...], inverse_low[...])
            solved_ref[k] = refined(basis_ref[k].reshape(full, n), inverse, matrix_ref)
        if k in staged:
            move["far_gram"].wait_recv()
            move["gram"] = spread_chip(sib_q.at[0:1, rank, mine], sib_q.at[0:1, rank, mine])
        if k > 0 and inner > 1:
            move["far_rest"].wait_recv()
            rest = spread(sib_q.at[1:inner, rank, mine], sib_q.at[1:inner, rank, mine])
        landed(move.get("own", []))
        landed(move["gram"])

        gram_own = own_q[0].reshape(full, full)
        gram_sib = sib_q[0].reshape(full, full)
        pair_ref[:full] = ident
        pair_ref[full:] = exact_dot(gram_sib, gram_own)

        def square(times):
            @pl.loop(0, times)
            def _(_):
                both = exact_dot(pair_ref[...], pair_ref[full:])
                pair_ref[:full] = pair_ref[:full] + both[:full]
                pair_ref[full:] = both[full:]

        square(squarings[0])
        near = []
        if k == 0:
            rest = move["rest"]
        else:
            shared = []
            for ref, group in ((own_q, move["own_rest"]), (sib_q, rest)):
                if inner > 1:
                    landed(group)
                    shared.append(push(ref.at[1:inner, :, mine], ref.at[1:inner, :, mine], other_core, rank))
            rest = shared
            near.append(share_far(k, 0))
        square(squarings[1])
        if k > 0 and after2 < blocks:
            near.append(share_far(k, 1))
        landed(rest)
        if k == 0:
            move["bulk"].wait_recv()
        else:
            near[0].wait_recv()

        solver = split(pair_ref[:full])
        own_parts, sib_parts = split(gram_own), split(gram_sib)
        proj_own = now[1 : inner + 1].reshape(inner * width, full)
        if inner > 1:
            sib_rows = [sib_q[1:inner, pl.ds(rank, 1)].reshape((inner - 1) * width, full), sib[inner]]
            proj_sib = jnp.concatenate(sib_rows, axis=0)
        else:
            proj_sib = sib[inner]
        target = proj_sib - dot3(split(proj_own), sib_parts)
        z_own = dot3(split(target), solver, NT)
        tail_weights[k] = z_own[(inner - 1) * width :]
        if inner > 1:
            z_sib = proj_own - dot3(split(z_own), own_parts)
            z_both = jnp.concatenate([z_own, z_sib], axis=1)
            after_rows = current[k + 1]
            at = 0
            for j in range(1, inner):
                if j == 2 and k > 0 and after2 < blocks:
                    near[1].wait_recv()
                count = inner + 1 - j
                q_own = own_q[j].reshape(full, full)
                q_sib = sib_q[j].reshape(full, full)
                q_both = jnp.concatenate([q_own, q_sib], axis=1)
                change = dot3(split(z_both[(j - 1) * width :]), split(q_both), NT)
                lo = after + at
                summed = now[lo : lo + count] + sib[lo : lo + count]
                after_rows[at : at + count] = summed - change.reshape(count, width, full)
                at += count
                if j == 1:
                    begin_column(k + 1)
            begin_rest(k + 1)
            rows = (inner - 1) * full
            q_own = own_q[1:inner].reshape(rows, full)
            q_sib = sib_q[1:inner].reshape(rows, full)
            wide = q_sib - dot3(split(q_own), sib_parts)
            weights[k][...] = dot3(split(wide), solver, NT)

    for k in reversed(range(levels)):
        value = tail_weights[k]
        for j in range(k + 1, levels):
            block = weights[k][(j - k - 1) * full : (j - k) * full]
            value = value - exact_dot(coefs_ref[j], block)
        coefs_ref[k] = value
    coefs = jnp.concatenate([coefs_ref[k] for k in range(levels)], axis=1)
    whole = split(solved_ref[...].reshape(levels * full, n))
    out_ref[...] = solved_sides[...] - dot3(split(coefs), whole)
    for copy in copies:
        copy.wait_send()


def tree_solve(points, bases, mask, right_sides, ranks):
    levels, width, n = bases.shape
    full = width * ranks
    starts = [0]
    for j in range(levels):
        starts.append(starts[-1] + levels + 1 - j)
    total = starts[-1]
    scratch = []
    for _ in range(2):
        for k in range(levels):
            scratch.append(pltpu.VMEM((total - starts[k], width, full), f32))
    for _ in range(2):
        for k in range(levels):
            scratch.append(pltpu.VMEM((levels - k, ranks, width, full), f32))
    for k in range(levels - 1):
        scratch.append(pltpu.VMEM(((levels - k - 1) * full, full), f32))
    scratch += [
        pltpu.VMEM((levels, width, full), f32),
        pltpu.VMEM((2 * full, full), f32),
        pltpu.VMEM((levels, width, full), f32),
        pltpu.VMEM((levels, ranks, width, n), f32),
        pltpu.VMEM((2, n, 128), f32),
        pltpu.VMEM((n, n), f32),
        pltpu.VMEM((n, n), f32),
        pltpu.VMEM((n, n), bf16),
        pltpu.VMEM((n, n), bf16),
        pltpu.VMEM((levels, full, n), f32),
        pltpu.VMEM((width, n), f32),
    ]
    limit = levels * 7 * ranks
    scratch += [pltpu.SemaphoreType.DMA((limit,)), pltpu.SemaphoreType.DMA((limit,))]
    return pl.pallas_call(
        functools.partial(tree_kernel, levels, ranks, width),
        out_shape=jax.ShapeDtypeStruct(right_sides.shape, f32),
        in_specs=[pl.BlockSpec(memory_space=pltpu.VMEM)] * 4,
        out_specs=pl.BlockSpec(memory_space=pltpu.VMEM),
        scratch_shapes=scratch,
        compiler_params=pltpu.CompilerParams(
            collective_id=0, has_side_effects=True, vmem_limit_bytes=60 << 20
        ),
    )(points, bases, mask, right_sides)


def local(points, bases, ranks, right_sides):
    width = bases.shape[1]
    n_ranks = lax.axis_size("rank")
    leaf_idx = lax.axis_index("leaf")
    rank_idx = lax.axis_index("rank")
    own_ranks = lax.dynamic_slice_in_dim(ranks, leaf_idx, 1, 1)
    columns = rank_idx * width + jnp.arange(width, dtype=jnp.int32)
    own_mask = (columns[None, :] < own_ranks).astype(f32)
    return tree_solve(points, bases, own_mask[:, :, None], right_sides, n_ranks)


def solution(mesh):
    placed = (P(None, "leaf"), P(None, "rank", "leaf"), P(), P("rank", "leaf"))
    return jax.shard_map(
        local, mesh=mesh, in_specs=placed, out_specs=P("rank", "leaf"), check_vma=False
    )
```
